512 devices in a mesh: row: 64 (over x, y, core), col: 8 (over z).
Axes of the slice: x: 4, y: 8, z: 8, core: 2. Of those that a mesh axis runs over, the one named last changes fastest.
Arguments:
- panel: bfloat16 [262144, 256], P('row'), may hold values from -400 to 400, as said below
- slab: bfloat16 [262144, 1024], P('row', 'col'), may hold values from -300 to 300
Outputs:
- factor: float32 [256, 256], P(None, 'col')
- coupling: float32 [256, 1024], P(None, 'col')
- remainder: bfloat16 [262144, 1024], P('row', 'col')
The draws below stay inside these ranges and needn't reach their ends.
Inputs may be any that keep to these rules, and one draw needn't show every extreme that they name: panel has full column rank.
All inputs are finite; a program needn't handle non-finite values.
Results may differ from the reference program's by a relative error of at most 0.015.
The reference program's roundings to bfloat16 on the way (of `update`) count: a program that leaves them out, or rounds other values in their place, can miss the bound.
Values sent between devices are 32-bit elements; how exact they have to be, the bound alone decides.
No kernel may reach another device: no remote copies, remote signals or barrier semaphores. Data moves between devices by JAX's collectives and lax.ppermute only.
A program may use at most 64 MiB of HBM per device.

```python
import jax
import jax.numpy as jnp
from jax import lax

K = 256
SLAB = 1024
M = 262144


def panel_values(key):
    base = jax.random.fold_in(key, 7)
    keys = jax.random.split(base, 3)
    raw = jax.random.normal(keys[0], (M, K), jnp.float32)
    mixing = jnp.eye(K, dtype=jnp.float32) + 0.5 * jax.random.normal(keys[1], (K, K), jnp.float32) / jnp.sqrt(K * 1.0)
    column_scale = jnp.exp(jax.random.uniform(keys[2], (K,), jnp.float32, jnp.log(0.5), jnp.log(2.0)))
    trend = 1.0 + 2.0 * jnp.arange(M, dtype=jnp.float32) / M
    row_scale = trend
    values = jnp.dot(raw, mixing) * column_scale[None, :] * row_scale[:, None]
    return jnp.clip(values, -400.0, 400.0)


def draw_panel(key, part):
    return panel_values(key).astype(jnp.bfloat16)


def draw_slab(key, part):
    values = panel_values(key)
    keys = jax.random.split(jax.random.fold_in(key, 13), 2)
    mixing = jax.random.normal(keys[0], (K, SLAB), jnp.float32) / jnp.sqrt(K * 1.0)
    noise = 0.5 * jax.random.normal(keys[1], (M, SLAB), jnp.float32)
    return jnp.clip(jnp.dot(values, mixing) + noise, -300.0, 300.0).astype(jnp.bfloat16)


def setup_inputs(seed: int = 0) -> dict:
    streams_of = jax.random.split(jax.random.key(seed), 3)
    return {
        "panel": draw_panel(jax.random.fold_in(streams_of[2], 71), 0),
        "slab": draw_slab(jax.random.fold_in(streams_of[2], 71), 0),
    }


def reference(panel, slab):
    total_rows = panel.shape[0]
    wide_panel = panel.astype(jnp.float32)
    wide_slab = slab.astype(jnp.float32)
    gram = jnp.dot(wide_panel.T, wide_panel, precision=lax.Precision.HIGHEST) / total_rows
    factor = jnp.linalg.cholesky(gram).T
    cross = jnp.dot(wide_panel.T, wide_slab, precision=lax.Precision.HIGHEST) / total_rows
    coupling = lax.linalg.triangular_solve(factor, cross, left_side=True, lower=False, transpose_a=True)
    update = lax.linalg.triangular_solve(factor, coupling, left_side=True, lower=False, transpose_a=False)
    update = update.astype(jnp.bfloat16)
    remainder = (wide_slab - jnp.dot(panel.astype(jnp.float32), update.astype(jnp.float32), preferred_element_type=jnp.float32)).astype(jnp.bfloat16)
    return (factor, coupling, remainder)
```

```python
import jax
import jax.numpy as jnp
from jax import lax
from jax.experimental import pallas as pl
from jax.experimental.pallas import tpu as pltpu
from jax.sharding import PartitionSpec as P

NB=32
def hdot(a,b,dims):
    return lax.dot_general(a,b,(dims,((),())),precision=lax.Precision.HIGHEST,preferred_element_type=jnp.float32)

def eliminate(m):
    nb=m.shape[0]
    rows=lax.broadcasted_iota(jnp.int32,m.shape,0)
    cols=lax.broadcasted_iota(jnp.int32,m.shape,1)
    for k in range(0,nb,2):
        r1=m[k:k+1,:]; r2=m[k+1:k+2,:]
        c1=jnp.broadcast_to(m[:,k:k+1],m.shape); c2=jnp.broadcast_to(m[:,k+1:k+2],m.shape)
        a=c1[k:k+1,:]; b=c2[k:k+1,:]; c=c2[k+1:k+2,:]
        inv=1.0/(a*c-b*b)
        r2n = r2-(b/a)*r1
        g1=(c*r1-b*r2)*inv
        g2=(a*r2-b*r1)*inv
        upd = m - c1*g1 - c2*g2
        m = jnp.where(rows>k+1, upd, jnp.where(rows==k+1, r2n, m))
    d=jnp.sum(jnp.where(rows==cols,m,0.0),axis=1,keepdims=True)
    m=m*lax.rsqrt(d)
    return jnp.where((cols>=nb)|(cols>=rows),m,0.0)

def chol_kernel(g_ref, r_ref, wt_ref, a_ref, b_ref):
    n=g_ref.shape[0]; nb=NB
    a_ref[...]=g_ref[...]
    eye=(lax.broadcasted_iota(jnp.int32,(nb,nb),0)==lax.broadcasted_iota(jnp.int32,(nb,nb),1)).astype(jnp.float32)
    r_ref[...]=jnp.zeros_like(r_ref)
    wt_ref[...]=jnp.zeros_like(wt_ref)
    b_ref[...]=jnp.zeros_like(b_ref)
    for i in range(n//nb):
        lo,hi=i*nb,(i+1)*nb
        m=jnp.concatenate([a_ref[lo:hi,lo:hi],eye],axis=1)
        m=eliminate(m)
        R=m[:,:nb]; Wt=m[:,nb:]
        r_ref[lo:hi,lo:hi]=R
        wt_ref[lo:hi,lo:hi]=Wt
        if lo>0:
            tb=hdot(Wt,b_ref[lo:hi,:lo],((1,),(0,)))
            wt_ref[lo:hi,:lo]=tb
        if hi<n:
            ta=hdot(Wt,a_ref[lo:hi,hi:],((1,),(0,)))
            r_ref[lo:hi,hi:]=ta
            a_ref[hi:,hi:]-=hdot(ta,ta,((0,),(0,)))
            b_ref[hi:,:hi]-=hdot(ta,wt_ref[lo:hi,:hi],((0,),(0,)))
def chol(g):
    n=g.shape[0]
    s=jax.ShapeDtypeStruct((n,n),jnp.float32)
    return pl.pallas_call(chol_kernel,out_shape=(s,s),scratch_shapes=[pltpu.VMEM((n,n),jnp.float32)]*2,name="chol")(g)


def exchange(parts):
    return lax.all_to_all(parts, "row", 0, 0, tiled=True)


def total(parts):
    mine = jnp.sum(exchange(parts), axis=0)
    return exchange(jnp.broadcast_to(mine[None], parts.shape))


def on_device(panel, slab):
    rows = lax.axis_size("row")
    scale = 1.0 / (panel.shape[0] * rows)
    contract = (((0,), (0,)), ((), ()))
    local_gram = lax.dot_general(panel, panel, contract, preferred_element_type=jnp.float32) * scale
    local_cross = lax.dot_general(panel, slab, contract, preferred_element_type=jnp.float32) * scale
    order, width = local_cross.shape
    tiles = local_gram.reshape(order // 8, 8, order // 128, 128).transpose(0, 2, 1, 3)
    tiles = total(tiles.reshape(rows, -1, 128)).reshape(tiles.shape)
    gram = tiles.transpose(0, 2, 1, 3).reshape(order, order)
    cross = total(local_cross.reshape(rows, -1, 128)).reshape(order, width)
    factor, inv_t = chol(gram)
    coupling = hdot(inv_t, cross, ((1,), (0,)))
    update = hdot(inv_t, coupling, ((0,), (0,))).astype(jnp.bfloat16)
    remainder = (
        slab.astype(jnp.float32) - jnp.dot(panel, update, preferred_element_type=jnp.float32)
    ).astype(jnp.bfloat16)
    share = factor.shape[1] // lax.axis_size("col")
    factor_part = lax.dynamic_slice_in_dim(factor, lax.axis_index("col") * share, share, 1)
    return (factor_part, coupling, remainder)


def solution(mesh):
    return jax.shard_map(
        on_device,
        mesh=mesh,
        in_specs=(P("row", None), P("row", "col")),
        out_specs=(P(None, "col"), P(None, "col"), P("row", "col")),
        check_vma=False,
    )
```

```python
import functools
import jax
import jax.numpy as jnp
from jax import lax
from jax.experimental import pallas as pl
from jax.experimental.pallas import tpu as pltpu
from jax.sharding import PartitionSpec as P

NB = 64


def hdot(a, b, dims):
    return lax.dot_general(
        a, b, (dims, ((), ())), precision=lax.Precision.HIGHEST, preferred_element_type=jnp.float32
    )


def row_of(x, s):
    return jnp.broadcast_to(x[s : s + 1, :], x.shape)


def eliminate(m, off, u_ref):
    count = m.shape[0] // 8
    g = [m[8 * i : 8 * i + 8, :] for i in range(count)]

    def lanes(x, j):
        return jnp.broadcast_to(x[:, off + j : off + j + 1], x.shape)

    c1 = [lanes(x, 0) for x in g]
    c2 = [lanes(x, 1) for x in g]
    for k in range(0, m.shape[0], 2):
        h, s = divmod(k, 8)
        r1, r2 = row_of(g[h], s), row_of(g[h], s + 1)
        a, b, c = row_of(c1[h], s), row_of(c2[h], s), row_of(c2[h], s + 1)
        ratio = b / a
        u_ref[k : k + 1, :] = (r1 * lax.rsqrt(a))[s : s + 1, :]
        u_ref[k + 1 : k + 2, :] = ((r2 - ratio * r1) * lax.rsqrt(c - b * ratio))[s + 1 : s + 2, :]
        if k + 2 == m.shape[0]:
            break
        inv = 1.0 / (a * c - b * b)
        p1, p2, p3 = c * inv, b * inv, a * inv
        h, t = divmod(k + 2, 8)
        v1, v2 = row_of(c1[h], t), row_of(c2[h], t)
        w1, w2 = row_of(c1[h], t + 1), row_of(c2[h], t + 1)
        x1, x2 = p1 * v1 - p2 * v2, p3 * v2 - p2 * v1
        y1, y2 = p1 * w1 - p2 * w2, p3 * w2 - p2 * w1
        g1, g2 = p1 * r1 - p2 * r2, p3 * r2 - p2 * r1
        for i in range(h, count):
            n1 = lanes(g[i], k + 2) - c1[i] * x1 - c2[i] * x2
            n2 = lanes(g[i], k + 3) - c1[i] * y1 - c2[i] * y2
            g[i] = g[i] - c1[i] * g1 - c2[i] * g2
            c1[i], c2[i] = n1, n2


def gather_kernel(scale, panel_ref, slab_ref, out_ref, gram, cross):
    step = pl.program_id(0)

    @pl.when(step == 0)
    def _():
        gram[...] = jnp.zeros_like(gram)
        cross[...] = jnp.zeros_like(cross)

    contract = (((0,), (0,)), ((), ()))
    panel = panel_ref[...]
    gram[...] += lax.dot_general(panel, panel, contract, preferred_element_type=jnp.float32)
    cross[...] += lax.dot_general(panel, slab_ref[...], contract, preferred_element_type=jnp.float32)

    @pl.when(step == pl.num_programs(0) - 1)
    def _():
        out_ref[:, 0:256] = gram[0:64, :] * scale
        out_ref[:, 256:384] = gram[64:128, 128:256] * scale
        out_ref[:, 384:512] = gram[128:192, 128:256] * scale
        lane = lax.broadcasted_iota(jnp.int32, (64, 128), 1)
        out_ref[:, 512:640] = jnp.where(lane >= 64, gram[64:128, 0:128], pltpu.roll(gram[192:256, 128:256], 64, 1)) * scale
        for i in range(4):
            out_ref[:, 640 + 128 * i : 768 + 128 * i] = cross[64 * i : 64 * i + 64, :] * scale


def local_sums(panel, slab, scale, chunk=1024):
    rows = panel.shape[0]
    return pl.pallas_call(
        functools.partial(gather_kernel, scale),
        grid=(rows // chunk,),
        in_specs=[pl.BlockSpec((chunk, 256), lambda i: (i, 0)), pl.BlockSpec((chunk, 128), lambda i: (i, 0))],
        out_specs=pl.BlockSpec((64, 1152), lambda i: (0, 0)),
        out_shape=jax.ShapeDtypeStruct((64, 1152), jnp.float32),
        scratch_shapes=[pltpu.VMEM((256, 256), jnp.float32), pltpu.VMEM((256, 128), jnp.float32)],
        name="sums",
    )(panel, slab)


CHUNKS = 8


def finish_kernel(which_ref, s_ref, panel_hbm, slab_hbm, l_ref, coup_ref, rem_hbm,
                  panel, slab, rem, x, t, r, u, sems):
    loads = [pltpu.make_async_copy(panel_hbm, panel, sems.at[0]), pltpu.make_async_copy(slab_hbm, slab, sems.at[1])]
    for load in loads:
        load.start()
    lane = lax.broadcasted_iota(jnp.int32, (64, 128), 1)
    sub = lax.broadcasted_iota(jnp.int32, (64, 128), 0)
    low = lane < 64
    eyes = [(lane == sub).astype(jnp.float32), (lane == sub + 64).astype(jnp.float32)]
    x[0:64, 0:256] = s_ref[:, 0:256]
    x[64:128, 128:256] = s_ref[:, 256:384]
    x[64:128, 0:128] = s_ref[:, 512:640]
    x[128:192, 128:256] = s_ref[:, 384:512]
    x[192:256, 128:256] = pltpu.roll(s_ref[:, 512:640], 64, 1)
    for i in range(4):
        x[64 * i : 64 * i + 64, 256:384] = s_ref[:, 640 + 128 * i : 768 + 128 * i]
        for j in range(2):
            x[64 * i : 64 * i + 64, 384 + 128 * j : 512 + 128 * j] = eyes[i % 2] if i // 2 == j else jnp.zeros((64, 128), jnp.float32)
    r[...] = jnp.zeros_like(r)
    update = jnp.zeros((256, 128), jnp.float32)
    for i in range(4):
        lo, hi = 64 * i, 64 * i + 64
        tile, off = lo // 128 * 128, lo % 128
        d = x[lo:hi, tile : tile + 128]
        m = jnp.where(low, d, eyes[1]) if off == 0 else jnp.where(low, eyes[0], d)
        eliminate(m, off, u)
        v = u[...]
        wt = v[:, 64 - off : 128 - off]
        start, end = hi // 128 * 128, 384 + (hi + 127) // 128 * 128
        ti = hdot(wt, x[lo:hi, start:end], ((1,), (0,)))
        t[lo:hi, start:end] = ti
        own = jnp.where((lane - off >= sub) & ((lane >= 64) == (off > 0)), v, 0.0)
        if off == 0:
            own = jnp.where(low, own, t[lo:hi, tile : tile + 128])
        r[lo:hi, tile : tile + 128] = own
        if tile == 0:
            r[lo:hi, 128:256] = t[lo:hi, 128:256]
        if hi < 256:
            down = hdot(ti[:, 0 : 256 - start], ti, ((0,), (0,)))
            x[hi:256, start:end] -= down[hi - start :, :]
        coup = t[lo:hi, 256:384]
        coup_ref[lo:hi, :] = coup
        wide = end - 384
        part = hdot(t[lo:hi, 384:end], coup, ((0,), (0,)))
        if wide < 256:
            update = update + jnp.concatenate([part, jnp.zeros((256 - wide, 128), jnp.float32)], axis=0)
        else:
            update = update + part
    update = update.astype(jnp.bfloat16)
    for load in loads:
        load.wait()
    step = panel.shape[0] // CHUNKS
    stores = []
    for i in range(CHUNKS):
        at = pl.ds(i * step, step)
        rem[at, :] = (
            slab[at, :].astype(jnp.float32) - jnp.dot(panel[at, :], update, preferred_element_type=jnp.float32)
        ).astype(jnp.bfloat16)
        store = pltpu.make_async_copy(rem.at[at, :], rem_hbm.at[at, :], sems.at[2 + i])
        store.start()
        stores.append(store)
    share = l_ref.shape[0]
    pick = lax.broadcasted_iota(jnp.int32, (share, 256), 1) == (
        lax.broadcasted_iota(jnp.int32, (share, 256), 0) + which_ref[0] * share
    )
    l_ref[...] = hdot(pick.astype(jnp.float32), r[...], ((1,), (1,)))
    for store in stores:
        store.wait()


def finish(which, sums, panel, slab, share):
    rows = panel.shape[0]
    vmem = pl.BlockSpec(memory_space=pltpu.VMEM)
    hbm = pl.BlockSpec(memory_space=pl.ANY)
    return pl.pallas_call(
        finish_kernel,
        in_specs=[pl.BlockSpec(memory_space=pltpu.SMEM), vmem, hbm, hbm],
        out_specs=(vmem, vmem, hbm),
        out_shape=(
            jax.ShapeDtypeStruct((share, 256), jnp.float32),
            jax.ShapeDtypeStruct((256, 128), jnp.float32),
            jax.ShapeDtypeStruct((rows, 128), jnp.bfloat16),
        ),
        scratch_shapes=[
            pltpu.VMEM((rows, 256), jnp.bfloat16),
            pltpu.VMEM((rows, 128), jnp.bfloat16),
            pltpu.VMEM((rows, 128), jnp.bfloat16),
            pltpu.VMEM((256, 640), jnp.float32),
            pltpu.VMEM((256, 640), jnp.float32),
            pltpu.VMEM((256, 256), jnp.float32),
            pltpu.VMEM((64, 128), jnp.float32),
            pltpu.SemaphoreType.DMA((2 + CHUNKS,)),
        ],
        compiler_params=pltpu.CompilerParams(vmem_limit_bytes=32 * 1024 * 1024),
        name="finish",
    )(which, sums, panel, slab)


def exchange(parts):
    return lax.all_to_all(parts, "row", 0, 0, tiled=True)


def on_device(panel, slab):
    rows = lax.axis_size("row")
    parts = exchange(local_sums(panel, slab, 1.0 / (panel.shape[0] * rows)))
    mine = jnp.sum(parts, axis=0, keepdims=True)
    sums = exchange(jnp.broadcast_to(mine, parts.shape))
    share = panel.shape[1] // lax.axis_size("col")
    which = lax.axis_index("col").astype(jnp.int32).reshape(1)
    lower, coupling, remainder = finish(which, sums, panel, slab, share)
    return (lower.T, coupling, remainder)


def solution(mesh):
    return jax.shard_map(
        on_device,
        mesh=mesh,
        in_specs=(P("row", None), P("row", "col")),
        out_specs=(P(None, "col"), P(None, "col"), P("row", "col")),
        check_vma=False,
    )
```

```python
import functools
import jax
import jax.numpy as jnp
from jax import lax
from jax.experimental import pallas as pl
from jax.experimental.pallas import tpu as pltpu
from jax.sharding import PartitionSpec as P

NB = 64


def hdot(a, b, dims):
    return lax.dot_general(
        a, b, (dims, ((), ())), precision=lax.Precision.HIGHEST, preferred_element_type=jnp.float32
    )


def row_of(x, s):
    return jnp.broadcast_to(x[s : s + 1, :], x.shape)


def eliminate(m, off, u_ref):
    count = m.shape[0] // 8
    g = [m[8 * i : 8 * i + 8, :] for i in range(count)]

    def lanes(x, j):
        return jnp.broadcast_to(x[:, off + j : off + j + 1], x.shape)

    ahead = [lanes(g[0], j) for j in range(8)]
    for h in range(count):
        cols = {h: ahead}
        if h + 1 < count:
            cols[h + 1] = [lanes(g[h + 1], 8 * h + j) for j in range(8)]
            ahead = [lanes(g[h + 1], 8 * h + 8 + j) for j in range(8)]
        rows = [row_of(g[h], r) for r in range(8)]
        invs, mults, scaled = [], [], []
        for j in range(8):
            pivot = row_of(cols[h][j], j)
            inv = 1.0 / pivot
            mult = {r: row_of(cols[h][j], r) * inv for r in range(j + 1, 8)}
            for r in range(j + 1, 8):
                cols[h][r] = cols[h][r] - cols[h][j] * mult[r]
            for r in range(j + 1, 8):
                rows[r] = rows[r] - mult[r] * rows[j]
            if h + 1 < count:
                for r in range(j + 1, 8):
                    cols[h + 1][r] = cols[h + 1][r] - cols[h + 1][j] * mult[r]
                ahead = [x - cols[h + 1][j] * (row_of(cols[h + 1][j], n) * inv) for n, x in enumerate(ahead)]
            scaled.append(rows[j] * inv)
            mults.append(mult)
            u_ref[8 * h + j : 8 * h + j + 1, :] = (rows[j] * lax.rsqrt(pivot))[j : j + 1, :]
        for i in range(h + 1, count):
            if i > h + 1:
                cols[i] = [lanes(g[i], 8 * h + j) for j in range(8)]
                for j in range(8):
                    for r in range(j + 1, 8):
                        cols[i][r] = cols[i][r] - cols[i][j] * mults[j][r]
            terms = [cols[i][j] * scaled[j] for j in range(8)]
            while len(terms) > 1:
                terms = [terms[n] + terms[n + 1] for n in range(0, len(terms), 2)]
            g[i] = g[i] - terms[0]


def gather_kernel(scale, groups, panel_hbm, slab_hbm, out, panel, slab, acc, sems):
    pieces = sum(groups)
    step = panel.shape[0] // pieces
    copies = []
    for i in range(pieces):
        at = pl.ds(i * step, step)
        pair = (
            pltpu.make_async_copy(panel_hbm.at[at, :], panel.at[at, :], sems.at[2 * i]),
            pltpu.make_async_copy(slab_hbm.at[at, :], slab.at[at, :], sems.at[2 * i + 1]),
        )
        for copy in pair:
            copy.start()
        copies.append(pair)
    contract = (((0,), (0,)), ((), ()))
    first = 0
    for n, size in enumerate(groups):
        for pair in copies[first : first + size]:
            for copy in pair:
                copy.wait()
        lo, hi = first * step, (first + size) * step
        first += size
        left = panel[lo:hi, :]
        right = jnp.concatenate([left, slab[lo:hi, :]], axis=1)
        top = lax.dot_general(left[:, :128], right, contract, preferred_element_type=jnp.float32)
        low = lax.dot_general(left[:, 128:], right[:, 128:], contract, preferred_element_type=jnp.float32)
        if n == 0:
            acc[0:128, :] = top
            acc[128:256, 128:384] = low
        else:
            acc[0:128, :] += top
            acc[128:256, 128:384] += low
    out[:, 0, 0:256] = acc[0:64, 0:256] * scale
    out[:, 0, 256:384] = acc[64:128, 128:256] * scale
    out[:, 0, 384:512] = acc[128:192, 128:256] * scale
    lane = lax.broadcasted_iota(jnp.int32, (64, 128), 1)
    out[:, 0, 512:640] = jnp.where(lane >= 64, acc[64:128, 0:128], pltpu.roll(acc[192:256, 128:256], 64, 1)) * scale
    for i in range(4):
        out[:, 0, 640 + 128 * i : 768 + 128 * i] = acc[64 * i : 64 * i + 64, 256:384] * scale


def local_sums(panel, slab, scale, groups=(2, 2)):
    rows = panel.shape[0]
    return pl.pallas_call(
        functools.partial(gather_kernel, scale, groups),
        in_specs=[pl.BlockSpec(memory_space=pl.ANY)] * 2,
        out_specs=pl.BlockSpec(memory_space=pltpu.VMEM),
        out_shape=jax.ShapeDtypeStruct((64, 1, 1152), jnp.float32),
        scratch_shapes=[
            pltpu.VMEM((rows, 256), jnp.bfloat16),
            pltpu.VMEM((rows, 128), jnp.bfloat16),
            pltpu.VMEM((256, 384), jnp.float32),
            pltpu.SemaphoreType.DMA((2 * sum(groups),)),
        ],
        compiler_params=pltpu.CompilerParams(vmem_limit_bytes=60 * 1024 * 1024),
        name="sums",
    )(panel, slab)


CHUNKS = 8


def finish_kernel(s_ref, panel_hbm, slab_hbm, l_ref, coup_ref, rem_hbm,
                  panel, slab, rem, x, t, r, u, sems):
    loads = [pltpu.make_async_copy(panel_hbm, panel, sems.at[0]), pltpu.make_async_copy(slab_hbm, slab, sems.at[1])]
    for load in loads:
        load.start()
    lane = lax.broadcasted_iota(jnp.int32, (64, 128), 1)
    sub = lax.broadcasted_iota(jnp.int32, (64, 128), 0)
    low = lane < 64
    eyes = [(lane == sub).astype(jnp.float32), (lane == sub + 64).astype(jnp.float32)]
    x[0:64, 0:256] = s_ref[:, 0:256]
    x[64:128, 128:256] = s_ref[:, 256:384]
    x[64:128, 0:128] = s_ref[:, 512:640]
    x[128:192, 128:256] = s_ref[:, 384:512]
    x[192:256, 128:256] = pltpu.roll(s_ref[:, 512:640], 64, 1)
    for i in range(4):
        x[64 * i : 64 * i + 64, 256:384] = s_ref[:, 640 + 128 * i : 768 + 128 * i]
        for j in range(2):
            x[64 * i : 64 * i + 64, 384 + 128 * j : 512 + 128 * j] = eyes[i % 2] if i // 2 == j else jnp.zeros((64, 128), jnp.float32)
    r[...] = jnp.zeros_like(r)
    def rest(i, v, wt):
        lo, hi = 64 * i, 64 * i + 64
        tile, off = lo // 128 * 128, lo % 128
        start, end = hi // 128 * 128, 384 + (hi + 127) // 128 * 128
        ti = hdot(wt, x[lo:hi, start:end], ((1,), (0,)))
        t[lo:hi, start:end] = ti
        own = jnp.where((lane - off >= sub) & ((lane >= 64) == (off > 0)), v, 0.0)
        if off == 0:
            own = jnp.where(low, own, t[lo:hi, tile : tile + 128])
        r[lo:hi, tile : tile + 128] = own
        if tile == 0:
            r[lo:hi, 128:256] = t[lo:hi, 128:256]
        if hi < 256:
            down = hdot(ti[:, 0 : 256 - start], ti, ((0,), (0,)))
            x[hi:256, start:end] -= down[hi - start :, :]
        coup = t[lo:hi, 256:384]
        coup_ref[lo:hi, :] = coup
        wide = end - 384
        part = hdot(t[lo:hi, 384:end], coup, ((0,), (0,)))
        if wide < 256:
            part = jnp.concatenate([part, jnp.zeros((256 - wide, 128), jnp.float32)], axis=0)
        return part

    def next_block(i, wt):
        lo, hi = 64 * i, 64 * i + 64
        tile, off = hi // 128 * 128, hi % 128
        ti = hdot(wt, x[lo:hi, tile : tile + 128], ((1,), (0,)))
        down = hdot(ti, ti, ((0,), (0,)))
        return x[hi : hi + 64, tile : tile + 128] - down[off : off + 64, :]

    update = None
    d = x[0:64, 0:128]
    held = None
    for i in range(4):
        m = jnp.where(low, d, eyes[1]) if i % 2 == 0 else jnp.where(low, eyes[0], d)
        eliminate(m, 64 * (i % 2), u.at[i])
        v = u[i]
        wt = v[:, 64:128] if i % 2 == 0 else v[:, 0:64]
        if held is not None:
            part = rest(*held)
            update = part if update is None else update + part
        if i < 3:
            d = next_block(i, wt)
        held = (i, v, wt)
    update = update + rest(*held)
    update = update.astype(jnp.bfloat16)
    for load in loads:
        load.wait()
    step = panel.shape[0] // CHUNKS
    stores = []
    for i in range(CHUNKS):
        at = pl.ds(i * step, step)
        rem[at, :] = (
            slab[at, :].astype(jnp.float32) - jnp.dot(panel[at, :], update, preferred_element_type=jnp.float32)
        ).astype(jnp.bfloat16)
        store = pltpu.make_async_copy(rem.at[at, :], rem_hbm.at[at, :], sems.at[2 + i])
        store.start()
        stores.append(store)
    share = l_ref.shape[0]
    pick = lax.broadcasted_iota(jnp.int32, (share, 256), 1) == (
        lax.broadcasted_iota(jnp.int32, (share, 256), 0) + lax.axis_index("col") * share
    )
    l_ref[...] = hdot(pick.astype(jnp.float32), r[...], ((1,), (1,)))
    for store in stores:
        store.wait()


def finish(sums, panel, slab, share):
    rows = panel.shape[0]
    vmem = pl.BlockSpec(memory_space=pltpu.VMEM)
    hbm = pl.BlockSpec(memory_space=pl.ANY)
    return pl.pallas_call(
        finish_kernel,
        in_specs=[vmem, hbm, hbm],
        out_specs=(vmem, vmem, hbm),
        out_shape=(
            jax.ShapeDtypeStruct((share, 256), jnp.float32),
            jax.ShapeDtypeStruct((256, 128), jnp.float32),
            jax.ShapeDtypeStruct((rows, 128), jnp.bfloat16),
        ),
        scratch_shapes=[
            pltpu.VMEM((rows, 256), jnp.bfloat16),
            pltpu.VMEM((rows, 128), jnp.bfloat16),
            pltpu.VMEM((rows, 128), jnp.bfloat16),
            pltpu.VMEM((256, 640), jnp.float32),
            pltpu.VMEM((256, 640), jnp.float32),
            pltpu.VMEM((256, 256), jnp.float32),
            pltpu.VMEM((4, 64, 128), jnp.float32),
            pltpu.SemaphoreType.DMA((2 + CHUNKS,)),
        ],
        compiler_params=pltpu.CompilerParams(vmem_limit_bytes=32 * 1024 * 1024),
        name="finish",
    )(sums, panel, slab)


def exchange(parts):
    return lax.all_to_all(parts, "row", 0, 0, tiled=True)


def on_device(panel, slab):
    rows = lax.axis_size("row")
    parts = exchange(local_sums(panel, slab, 1.0 / (panel.shape[0] * rows)))
    mine = jnp.sum(parts, axis=0, keepdims=True)
    sums = exchange(jnp.broadcast_to(mine, parts.shape))
    share = panel.shape[1] // lax.axis_size("col")
    lower, coupling, remainder = finish(sums.reshape(rows, -1), panel, slab, share)
    return (lower.T, coupling, remainder)


def solution(mesh):
    return jax.shard_map(
        on_device,
        mesh=mesh,
        in_specs=(P("row", None), P("row", "col")),
        out_specs=(P(None, "col"), P(None, "col"), P("row", "col")),
        check_vma=False,
    )
```

```python
import functools
import jax
import jax.numpy as jnp
from jax import lax
from jax.experimental import pallas as pl
from jax.experimental.pallas import tpu as pltpu
from jax.sharding import PartitionSpec as P

NB = 64


def hdot(a, b, dims):
    return lax.dot_general(
        a, b, (dims, ((), ())), precision=lax.Precision.HIGHEST, preferred_element_type=jnp.float32
    )


def row_of(x, s):
    return jnp.broadcast_to(x[s : s + 1, :], x.shape)


def eliminate(m, off, u_ref):
    count = m.shape[0] // 8
    g = [m[8 * i : 8 * i + 8, :] for i in range(count)]

    def lanes(x, j):
        return jnp.broadcast_to(x[:, off + j : off + j + 1], x.shape)

    ahead = [lanes(g[0], j) for j in range(8)]
    for h in range(count):
        near = {h: ahead}
        if h + 1 < count:
            near[h + 1] = [lanes(g[h + 1], 8 * h + j) for j in range(8)]
            ahead = [lanes(g[h + 1], 8 * h + 8 + j) for j in range(8)]
        mine = near[h]
        block = g[h]
        rows, invs, entries, shares = [], [], [], []
        for j in range(8):
            pivot = row_of(mine[j], j)
            inv = 1.0 / pivot
            entry = {r: row_of(mine[j], r) for r in range(j + 1, 8)}
            row = row_of(block, j)
            share = mine[j] * inv
            for r in range(j + 1, 8):
                mine[r] = mine[r] - share * entry[r]
            if j < 7:
                block = block - share * row
            if h + 1 < count:
                below = near[h + 1]
                part = below[j] * inv
                for r in range(j + 1, 8):
                    below[r] = below[r] - part * entry[r]
                ahead = [x - below[j] * row_of(part, n) for n, x in enumerate(ahead)]
                shares.append(part)
            u_ref[8 * h + j : 8 * h + j + 1, :] = (row * lax.rsqrt(pivot))[j : j + 1, :]
            rows.append(row)
            invs.append(inv)
            entries.append(entry)
        for i in range(h + 1, count):
            if i > h + 1:
                far = [lanes(g[i], 8 * h + j) for j in range(8)]
                shares = []
                for j in range(8):
                    part = far[j] * invs[j]
                    for r in range(j + 1, 8):
                        far[r] = far[r] - part * entries[j][r]
                    shares.append(part)
            terms = [share * row for share, row in zip(shares, rows)]
            while len(terms) > 1:
                terms = [terms[n] + terms[n + 1] for n in range(0, len(terms), 2)]
            g[i] = g[i] - terms[0]


def gather_kernel(scale, groups, panel_hbm, slab_hbm, out, panel, slab, acc, sems):
    pieces = sum(groups)
    step = panel.shape[0] // pieces
    copies = []
    for i in range(pieces):
        at = pl.ds(i * step, step)
        pair = (
            pltpu.make_async_copy(panel_hbm.at[at, :], panel.at[at, :], sems.at[2 * i]),
            pltpu.make_async_copy(slab_hbm.at[at, :], slab.at[at, :], sems.at[2 * i + 1]),
        )
        for copy in pair:
            copy.start()
        copies.append(pair)
    contract = (((0,), (0,)), ((), ()))
    first = 0
    for n, size in enumerate(groups):
        for pair in copies[first : first + size]:
            for copy in pair:
                copy.wait()
        lo, hi = first * step, (first + size) * step
        first += size
        left = panel[lo:hi, :]
        right = jnp.concatenate([left, slab[lo:hi, :]], axis=1)
        top = lax.dot_general(left[:, :128], right, contract, preferred_element_type=jnp.float32)
        low = lax.dot_general(left[:, 128:], right[:, 128:], contract, preferred_element_type=jnp.float32)
        if n == 0:
            acc[0:128, :] = top
            acc[128:256, 128:384] = low
        else:
            acc[0:128, :] += top
            acc[128:256, 128:384] += low
    out[:, 0, 0:256] = acc[0:64, 0:256] * scale
    out[:, 0, 256:384] = acc[64:128, 128:256] * scale
    out[:, 0, 384:512] = acc[128:192, 128:256] * scale
    lane = lax.broadcasted_iota(jnp.int32, (64, 128), 1)
    out[:, 0, 512:640] = jnp.where(lane >= 64, acc[64:128, 0:128], pltpu.roll(acc[192:256, 128:256], 64, 1)) * scale
    for i in range(4):
        out[:, 0, 640 + 128 * i : 768 + 128 * i] = acc[64 * i : 64 * i + 64, 256:384] * scale


def local_sums(panel, slab, scale, groups=(2, 2)):
    rows = panel.shape[0]
    return pl.pallas_call(
        functools.partial(gather_kernel, scale, groups),
        in_specs=[pl.BlockSpec(memory_space=pl.ANY)] * 2,
        out_specs=pl.BlockSpec(memory_space=pltpu.VMEM),
        out_shape=jax.ShapeDtypeStruct((64, 1, 1152), jnp.float32),
        scratch_shapes=[
            pltpu.VMEM((rows, 256), jnp.bfloat16),
            pltpu.VMEM((rows, 128), jnp.bfloat16),
            pltpu.VMEM((256, 384), jnp.float32),
            pltpu.SemaphoreType.DMA((2 * sum(groups),)),
        ],
        compiler_params=pltpu.CompilerParams(vmem_limit_bytes=60 * 1024 * 1024),
        name="sums",
    )(panel, slab)


CHUNKS = 4


def finish_kernel(s_ref, panel, slab, l_ref, coup_ref, rem_hbm,
                  rem, x, t, r, u, sems):
    lane = lax.broadcasted_iota(jnp.int32, (64, 128), 1)
    sub = lax.broadcasted_iota(jnp.int32, (64, 128), 0)
    low = lane < 64
    eyes = [(lane == sub).astype(jnp.float32), (lane == sub + 64).astype(jnp.float32)]
    x[0:64, 0:256] = s_ref[:, 0:256]
    x[64:128, 128:256] = s_ref[:, 256:384]
    x[64:128, 0:128] = s_ref[:, 512:640]
    x[128:192, 128:256] = s_ref[:, 384:512]
    x[192:256, 128:256] = pltpu.roll(s_ref[:, 512:640], 64, 1)
    for i in range(4):
        x[64 * i : 64 * i + 64, 256:384] = s_ref[:, 640 + 128 * i : 768 + 128 * i]
        for j in range(2):
            x[64 * i : 64 * i + 64, 384 + 128 * j : 512 + 128 * j] = eyes[i % 2] if i // 2 == j else jnp.zeros((64, 128), jnp.float32)
    r[...] = jnp.zeros_like(r)
    def keep(i, v):
        lo = 64 * i
        tile, off = lo // 128 * 128, lo % 128
        own = jnp.where((lane - off >= sub) & ((lane >= 64) == (off > 0)), v, 0.0)
        if off == 0:
            own = jnp.where(low, own, t[lo : lo + 64, tile : tile + 128])
        r[lo : lo + 64, tile : tile + 128] = own
        if tile == 0:
            r[lo : lo + 64, 128:256] = t[lo : lo + 64, 128:256]
        coup_ref[lo : lo + 64, :] = t[lo : lo + 64, 256:384]

    def solve(i, wt):
        lo, hi = 64 * i, 64 * i + 64
        start, end = hi // 128 * 128, 384 + (hi + 127) // 128 * 128
        t[lo:hi, start:end] = hdot(wt, x[lo:hi, start:end], ((1,), (0,)))

    def reduce(lo, hi, first, last, start, end):
        tile = first // 128 * 128
        down = hdot(t[lo:hi, tile : tile + 128], t[lo:hi, start:end], ((0,), (0,)))
        x[first:last, start:end] -= down[first - tile : last - tile, :]

    def backward(lo, hi):
        wide = (hi + 127) // 128 * 128
        part = hdot(t[lo:hi, 384 : 384 + wide], t[lo:hi, 256:384], ((0,), (0,)))
        if wide < 256:
            part = jnp.concatenate([part, jnp.zeros((256 - wide, 128), jnp.float32)], axis=0)
        return part

    def next_block(i, wt):
        lo, hi = 64 * i, 64 * i + 64
        tile, off = hi // 128 * 128, hi % 128
        t[lo:hi, tile : tile + 128] = hdot(wt, x[lo:hi, tile : tile + 128], ((1,), (0,)))
        ti = t[0:hi, 128:256] if i == 1 else t[lo:hi, tile : tile + 128]
        down = hdot(ti, ti, ((0,), (0,)))
        return x[hi : hi + 64, tile : tile + 128] - down[off : off + 64, :]

    d = x[0:64, 0:128]
    for i in range(4):
        m = jnp.where(low, d, eyes[1]) if i % 2 == 0 else jnp.where(low, eyes[0], d)
        eliminate(m, 64 * (i % 2), u.at[i])
        v = u[i]
        wt = v[:, 64:128] if i % 2 == 0 else v[:, 0:64]
        if i < 3:
            d = next_block(i, wt)
        solve(i, wt)
        if i == 0:
            reduce(0, 64, 64, 128, 128, 512)
        elif i == 1:
            reduce(0, 128, 128, 256, 128, 512)
            update = backward(0, 128)
        elif i == 2:
            reduce(128, 192, 192, 256, 256, 640)
            update = update + backward(128, 192)
        else:
            update = update + backward(192, 256)
        keep(i, v)
    update = update.astype(jnp.bfloat16)
    step = panel.shape[0] // CHUNKS
    stores = []
    for i in range(CHUNKS):
        at = pl.ds(i * step, step)
        rem[at, :] = (
            slab[at, :].astype(jnp.float32) - jnp.dot(panel[at, :], update, preferred_element_type=jnp.float32)
        ).astype(jnp.bfloat16)
        store = pltpu.make_async_copy(rem.at[at, :], rem_hbm.at[at, :], sems.at[i])
        store.start()
        stores.append(store)
    share = l_ref.shape[0]
    pick = lax.broadcasted_iota(jnp.int32, (share, 256), 1) == (
        lax.broadcasted_iota(jnp.int32, (share, 256), 0) + lax.axis_index("col") * share
    )
    l_ref[...] = hdot(pick.astype(jnp.float32), r[...], ((1,), (1,)))
    for store in stores:
        store.wait()


def finish(sums, panel, slab, share):
    rows = panel.shape[0]
    vmem = pl.BlockSpec(memory_space=pltpu.VMEM)
    hbm = pl.BlockSpec(memory_space=pl.ANY)
    return pl.pallas_call(
        finish_kernel,
        in_specs=[vmem, vmem, vmem],
        out_specs=(vmem, vmem, hbm),
        out_shape=(
            jax.ShapeDtypeStruct((share, 256), jnp.float32),
            jax.ShapeDtypeStruct((256, 128), jnp.float32),
            jax.ShapeDtypeStruct((rows, 128), jnp.bfloat16),
        ),
        scratch_shapes=[
            pltpu.VMEM((rows, 128), jnp.bfloat16),
            pltpu.VMEM((256, 640), jnp.float32),
            pltpu.VMEM((256, 640), jnp.float32),
            pltpu.VMEM((256, 256), jnp.float32),
            pltpu.VMEM((4, 64, 128), jnp.float32),
            pltpu.SemaphoreType.DMA((CHUNKS,)),
        ],
        compiler_params=pltpu.CompilerParams(vmem_limit_bytes=24 * 1024 * 1024),
        name="finish",
    )(sums, panel, slab)


def exchange(parts):
    return lax.all_to_all(parts, "row", 0, 0, tiled=True)


def on_device(panel, slab):
    rows = lax.axis_size("row")
    parts = exchange(local_sums(panel, slab, 1.0 / (panel.shape[0] * rows)))
    mine = jnp.sum(parts, axis=0, keepdims=True)
    sums = exchange(jnp.broadcast_to(mine, parts.shape))
    share = panel.shape[1] // lax.axis_size("col")
    lower, coupling, remainder = finish(sums.reshape(rows, -1), panel, slab, share)
    return (lower.T, coupling, remainder)


def solution(mesh):
    return jax.shard_map(
        on_device,
        mesh=mesh,
        in_specs=(P("row", None), P("row", "col")),
        out_specs=(P(None, "col"), P(None, "col"), P("row", "col")),
        check_vma=False,
    )
```

```python
import functools
import jax
import jax.numpy as jnp
from jax import lax
from jax.experimental import pallas as pl
from jax.experimental.pallas import tpu as pltpu
from jax.sharding import PartitionSpec as P

NB = 64


def hdot(a, b, dims):
    return lax.dot_general(
        a, b, (dims, ((), ())), precision=lax.Precision.HIGHEST, preferred_element_type=jnp.float32
    )


def row_of(x, s):
    return jnp.broadcast_to(x[s : s + 1, :], x.shape)


def eliminate(m, off, u_ref):
    count = m.shape[0] // 8
    g = [m[8 * i : 8 * i + 8, :] for i in range(count)]

    def lanes(x, j):
        return jnp.broadcast_to(x[:, off + j : off + j + 1], x.shape)

    ahead = [lanes(g[0], j) for j in range(8)]
    for h in range(count):
        near = {h: ahead}
        if h + 1 < count:
            near[h + 1] = [lanes(g[h + 1], 8 * h + j) for j in range(8)]
            ahead = [lanes(g[h + 1], 8 * h + 8 + j) for j in range(8)]
        mine = near[h]
        block = g[h]
        rows, invs, entries, shares = [], [], [], []
        for j in range(8):
            pivot = row_of(mine[j], j)
            inv = 1.0 / pivot
            entry = {r: row_of(mine[j], r) for r in range(j + 1, 8)}
            row = row_of(block, j)
            share = mine[j] * inv
            for r in range(j + 1, 8):
                mine[r] = mine[r] - share * entry[r]
            if j < 7:
                block = block - share * row
            if h + 1 < count:
                below = near[h + 1]
                part = below[j] * inv
                for r in range(j + 1, 8):
                    below[r] = below[r] - part * entry[r]
                ahead = [x - below[j] * row_of(part, n) for n, x in enumerate(ahead)]
                shares.append(part)
            u_ref[8 * h + j : 8 * h + j + 1, :] = (row * lax.rsqrt(pivot))[j : j + 1, :]
            rows.append(row)
            invs.append(inv)
            entries.append(entry)
        for i in range(h + 1, count):
            if i > h + 1:
                far = [lanes(g[i], 8 * h + j) for j in range(8)]
                shares = []
                for j in range(8):
                    part = far[j] * invs[j]
                    for r in range(j + 1, 8):
                        far[r] = far[r] - part * entries[j][r]
                    shares.append(part)
            terms = [share * row for share, row in zip(shares, rows)]
            while len(terms) > 1:
                terms = [terms[n] + terms[n + 1] for n in range(0, len(terms), 2)]
            g[i] = g[i] - terms[0]


def gather_kernel(scale, groups, panel_hbm, slab_hbm, out, panel, slab, acc, sems):
    pieces = sum(groups)
    step = panel.shape[0] // pieces
    copies = []
    for i in range(pieces):
        at = pl.ds(i * step, step)
        pair = (
            pltpu.make_async_copy(panel_hbm.at[at, :], panel.at[at, :], sems.at[2 * i]),
            pltpu.make_async_copy(slab_hbm.at[at, :], slab.at[at, :], sems.at[2 * i + 1]),
        )
        for copy in pair:
            copy.start()
        copies.append(pair)
    contract = (((0,), (0,)), ((), ()))
    first = 0
    for n, size in enumerate(groups):
        for pair in copies[first : first + size]:
            for copy in pair:
                copy.wait()
        lo, hi = first * step, (first + size) * step
        first += size
        left = panel[lo:hi, :]
        right = jnp.concatenate([left, slab[lo:hi, :]], axis=1)
        top = lax.dot_general(left[:, :128], right, contract, preferred_element_type=jnp.float32)
        low = lax.dot_general(left[:, 128:], right[:, 128:], contract, preferred_element_type=jnp.float32)
        if n == 0:
            acc[0:128, :] = top
            acc[128:256, 128:384] = low
        else:
            acc[0:128, :] += top
            acc[128:256, 128:384] += low
    out[:, 0, 0:256] = acc[0:64, 0:256] * scale
    out[:, 0, 256:384] = acc[64:128, 128:256] * scale
    out[:, 0, 384:512] = acc[128:192, 128:256] * scale
    lane = lax.broadcasted_iota(jnp.int32, (64, 128), 1)
    out[:, 0, 512:640] = jnp.where(lane >= 64, acc[64:128, 0:128], pltpu.roll(acc[192:256, 128:256], 64, 1)) * scale
    for i in range(4):
        out[:, 0, 640 + 128 * i : 768 + 128 * i] = acc[64 * i : 64 * i + 64, 256:384] * scale


def local_sums(panel, slab, scale, groups=(2, 2)):
    rows = panel.shape[0]
    return pl.pallas_call(
        functools.partial(gather_kernel, scale, groups),
        in_specs=[pl.BlockSpec(memory_space=pltpu.HBM)] * 2,
        out_specs=pl.BlockSpec(memory_space=pltpu.VMEM),
        out_shape=pltpu.VMEM((64, 1, 1152), jnp.float32),
        scratch_shapes=[
            pltpu.VMEM((rows, 256), jnp.bfloat16),
            pltpu.VMEM((rows, 128), jnp.bfloat16),
            pltpu.VMEM((256, 384), jnp.float32),
            pltpu.SemaphoreType.DMA((2 * sum(groups),)),
        ],
        compiler_params=pltpu.CompilerParams(vmem_limit_bytes=60 * 1024 * 1024),
        name="sums",
    )(panel, slab)


CHUNKS = 4


def finish_kernel(s_ref, panel, slab, l_hbm, coup_hbm, rem_hbm,
                  l_ref, coup_ref, rem, x, t, r, u, sems):
    lane = lax.broadcasted_iota(jnp.int32, (64, 128), 1)
    sub = lax.broadcasted_iota(jnp.int32, (64, 128), 0)
    low = lane < 64
    eyes = [(lane == sub).astype(jnp.float32), (lane == sub + 64).astype(jnp.float32)]
    x[0:64, 0:256] = s_ref[:, 0:256]
    x[64:128, 128:256] = s_ref[:, 256:384]
    x[64:128, 0:128] = s_ref[:, 512:640]
    x[128:192, 128:256] = s_ref[:, 384:512]
    x[192:256, 128:256] = pltpu.roll(s_ref[:, 512:640], 64, 1)
    for i in range(4):
        x[64 * i : 64 * i + 64, 256:384] = s_ref[:, 640 + 128 * i : 768 + 128 * i]
        for j in range(2):
            x[64 * i : 64 * i + 64, 384 + 128 * j : 512 + 128 * j] = eyes[i % 2] if i // 2 == j else jnp.zeros((64, 128), jnp.float32)
    r[...] = jnp.zeros_like(r)
    def keep(i, v):
        lo = 64 * i
        tile, off = lo // 128 * 128, lo % 128
        own = jnp.where((lane - off >= sub) & ((lane >= 64) == (off > 0)), v, 0.0)
        if off == 0:
            own = jnp.where(low, own, t[lo : lo + 64, tile : tile + 128])
        r[lo : lo + 64, tile : tile + 128] = own
        if tile == 0:
            r[lo : lo + 64, 128:256] = t[lo : lo + 64, 128:256]
        coup_ref[lo : lo + 64, :] = t[lo : lo + 64, 256:384]

    def solve(i, wt):
        lo, hi = 64 * i, 64 * i + 64
        start, end = hi // 128 * 128, 384 + (hi + 127) // 128 * 128
        t[lo:hi, start:end] = hdot(wt, x[lo:hi, start:end], ((1,), (0,)))

    def reduce(lo, hi, first, last, start, end):
        tile = first // 128 * 128
        down = hdot(t[lo:hi, tile : tile + 128], t[lo:hi, start:end], ((0,), (0,)))
        x[first:last, start:end] -= down[first - tile : last - tile, :]

    def backward(lo, hi):
        wide = (hi + 127) // 128 * 128
        part = hdot(t[lo:hi, 384 : 384 + wide], t[lo:hi, 256:384], ((0,), (0,)))
        if wide < 256:
            part = jnp.concatenate([part, jnp.zeros((256 - wide, 128), jnp.float32)], axis=0)
        return part

    def next_block(i, wt):
        lo, hi = 64 * i, 64 * i + 64
        tile, off = hi // 128 * 128, hi % 128
        t[lo:hi, tile : tile + 128] = hdot(wt, x[lo:hi, tile : tile + 128], ((1,), (0,)))
        ti = t[0:hi, 128:256] if i == 1 else t[lo:hi, tile : tile + 128]
        down = hdot(ti, ti, ((0,), (0,)))
        return x[hi : hi + 64, tile : tile + 128] - down[off : off + 64, :]

    d = x[0:64, 0:128]
    for i in range(4):
        m = jnp.where(low, d, eyes[1]) if i % 2 == 0 else jnp.where(low, eyes[0], d)
        eliminate(m, 64 * (i % 2), u.at[i])
        v = u[i]
        wt = v[:, 64:128] if i % 2 == 0 else v[:, 0:64]
        if i < 3:
            d = next_block(i, wt)
        solve(i, wt)
        if i == 0:
            reduce(0, 64, 64, 128, 128, 512)
        elif i == 1:
            reduce(0, 128, 128, 256, 128, 512)
            update = backward(0, 128)
        elif i == 2:
            reduce(128, 192, 192, 256, 256, 640)
            update = update + backward(128, 192)
        else:
            update = update + backward(192, 256)
        keep(i, v)
    update = update.astype(jnp.bfloat16)
    step = panel.shape[0] // CHUNKS
    share = l_ref.shape[0]
    pick = lax.broadcasted_iota(jnp.int32, (share, 256), 1) == (
        lax.broadcasted_iota(jnp.int32, (share, 256), 0) + lax.axis_index("col") * share
    )
    l_ref[...] = hdot(pick.astype(jnp.float32), r[...], ((1,), (1,)))
    stores = [
        pltpu.make_async_copy(l_ref, l_hbm, sems.at[CHUNKS]),
        pltpu.make_async_copy(coup_ref, coup_hbm, sems.at[CHUNKS + 1]),
    ]
    for store in stores:
        store.start()
    for i in range(CHUNKS):
        at = pl.ds(i * step, step)
        rem[at, :] = (
            slab[at, :].astype(jnp.float32) - jnp.dot(panel[at, :], update, preferred_element_type=jnp.float32)
        ).astype(jnp.bfloat16)
        store = pltpu.make_async_copy(rem.at[at, :], rem_hbm.at[at, :], sems.at[i])
        store.start()
        stores.append(store)
    for store in stores:
        store.wait()


def finish(sums, panel, slab, share):
    rows = panel.shape[0]
    vmem = pl.BlockSpec(memory_space=pltpu.VMEM)
    hbm = pl.BlockSpec(memory_space=pl.ANY)
    return pl.pallas_call(
        finish_kernel,
        in_specs=[vmem, vmem, vmem],
        out_specs=(hbm, hbm, hbm),
        out_shape=(
            jax.ShapeDtypeStruct((share, 256), jnp.float32),
            jax.ShapeDtypeStruct((256, 128), jnp.float32),
            jax.ShapeDtypeStruct((rows, 128), jnp.bfloat16),
        ),
        scratch_shapes=[
            pltpu.VMEM((share, 256), jnp.float32),
            pltpu.VMEM((256, 128), jnp.float32),
            pltpu.VMEM((rows, 128), jnp.bfloat16),
            pltpu.VMEM((256, 640), jnp.float32),
            pltpu.VMEM((256, 640), jnp.float32),
            pltpu.VMEM((256, 256), jnp.float32),
            pltpu.VMEM((4, 64, 128), jnp.float32),
            pltpu.SemaphoreType.DMA((CHUNKS + 2,)),
        ],
        compiler_params=pltpu.CompilerParams(vmem_limit_bytes=24 * 1024 * 1024),
        name="finish",
    )(sums, panel, slab)


def exchange(parts):
    return lax.all_to_all(parts, "row", 0, 0, tiled=True)


def on_device(panel, slab):
    rows = lax.axis_size("row")
    parts = exchange(local_sums(panel, slab, 1.0 / (panel.shape[0] * rows)))
    mine = jnp.sum(parts, axis=0, keepdims=True)
    sums = exchange(jnp.broadcast_to(mine, parts.shape))
    share = panel.shape[1] // lax.axis_size("col")
    lower, coupling, remainder = finish(sums.reshape(rows, -1), panel, slab, share)
    return (lower.T, coupling, remainder)


def solution(mesh):
    return jax.shard_map(
        on_device,
        mesh=mesh,
        in_specs=(P("row", None), P("row", "col")),
        out_specs=(P(None, "col"), P(None, "col"), P("row", "col")),
        check_vma=False,
    )
```

```python
import functools
import jax
import jax.numpy as jnp
from jax import lax
from jax.experimental import pallas as pl
from jax.experimental.pallas import tpu as pltpu
from jax.sharding import PartitionSpec as P

NB = 64


def hdot(a, b, dims):
    return lax.dot_general(
        a, b, (dims, ((), ())), precision=lax.Precision.HIGHEST, preferred_element_type=jnp.float32
    )


def row_of(x, s):
    return jnp.broadcast_to(x[s : s + 1, :], x.shape)


def eliminate(m, off, u_ref):
    count = m.shape[0] // 8
    g = [m[8 * i : 8 * i + 8, :] for i in range(count)]

    def lanes(x, j):
        return jnp.broadcast_to(x[:, off + j : off + j + 1], x.shape)

    ahead = [lanes(g[0], j) for j in range(8)]
    for h in range(count):
        near = {h: ahead}
        if h + 1 < count:
            near[h + 1] = [lanes(g[h + 1], 8 * h + j) for j in range(8)]
            ahead = [lanes(g[h + 1], 8 * h + 8 + j) for j in range(8)]
        mine = near[h]
        block = g[h]
        rows, invs, entries, shares = [], [], [], []
        for j in range(8):
            pivot = row_of(mine[j], j)
            inv = 1.0 / pivot
            entry = {r: row_of(mine[j], r) for r in range(j + 1, 8)}
            row = row_of(block, j)
            share = mine[j] * inv
            for r in range(j + 1, 8):
                mine[r] = mine[r] - share * entry[r]
            if j < 7:
                block = block - share * row
            if h + 1 < count:
                below = near[h + 1]
                part = below[j] * inv
                for r in range(j + 1, 8):
                    below[r] = below[r] - part * entry[r]
                ahead = [x - below[j] * row_of(part, n) for n, x in enumerate(ahead)]
                shares.append(part)
            u_ref[8 * h + j : 8 * h + j + 1, :] = (row * lax.rsqrt(pivot))[j : j + 1, :]
            rows.append(row)
            invs.append(inv)
            entries.append(entry)
        for i in range(h + 1, count):
            if i > h + 1:
                far = [lanes(g[i], 8 * h + j) for j in range(8)]
                shares = []
                for j in range(8):
                    part = far[j] * invs[j]
                    for r in range(j + 1, 8):
                        far[r] = far[r] - part * entries[j][r]
                    shares.append(part)
            terms = [share * row for share, row in zip(shares, rows)]
            while len(terms) > 1:
                terms = [terms[n] + terms[n + 1] for n in range(0, len(terms), 2)]
            g[i] = g[i] - terms[0]


def gather_kernel(scale, groups, panel_hbm, slab_hbm, out, panel, slab, acc, sems):
    pieces = sum(groups)
    step = panel.shape[0] // pieces
    copies = []
    for i in range(pieces):
        at = pl.ds(i * step, step)
        pair = (
            pltpu.make_async_copy(panel_hbm.at[at, :], panel.at[at, :], sems.at[2 * i]),
            pltpu.make_async_copy(slab_hbm.at[at, :], slab.at[at, :], sems.at[2 * i + 1]),
        )
        for copy in pair:
            copy.start()
        copies.append(pair)
    contract = (((0,), (0,)), ((), ()))
    first = 0
    for n, size in enumerate(groups):
        for pair in copies[first : first + size]:
            for copy in pair:
                copy.wait()
        lo, hi = first * step, (first + size) * step
        first += size
        left = panel[lo:hi, :]
        right = jnp.concatenate([left, slab[lo:hi, :]], axis=1)
        top = lax.dot_general(left[:, :128], right, contract, preferred_element_type=jnp.float32)
        low = lax.dot_general(left[:, 128:], right[:, 128:], contract, preferred_element_type=jnp.float32)
        if n == 0:
            acc[0:128, :] = top
            acc[128:256, 128:384] = low
        else:
            acc[0:128, :] += top
            acc[128:256, 128:384] += low
    out[:, 0, 0:256] = acc[0:64, 0:256] * scale
    out[:, 0, 256:384] = acc[64:128, 128:256] * scale
    out[:, 0, 384:512] = acc[128:192, 128:256] * scale
    lane = lax.broadcasted_iota(jnp.int32, (64, 128), 1)
    out[:, 0, 512:640] = jnp.where(lane >= 64, acc[64:128, 0:128], pltpu.roll(acc[192:256, 128:256], 64, 1)) * scale
    for i in range(4):
        out[:, 0, 640 + 128 * i : 768 + 128 * i] = acc[64 * i : 64 * i + 64, 256:384] * scale


def local_sums(panel, slab, scale, groups=(2, 2)):
    rows = panel.shape[0]
    return pl.pallas_call(
        functools.partial(gather_kernel, scale, groups),
        in_specs=[pl.BlockSpec(memory_space=pltpu.HBM)] * 2,
        out_specs=pl.BlockSpec(memory_space=pltpu.VMEM),
        out_shape=pltpu.VMEM((64, 1, 1152), jnp.float32),
        scratch_shapes=[
            pltpu.VMEM((rows, 256), jnp.bfloat16),
            pltpu.VMEM((rows, 128), jnp.bfloat16),
            pltpu.VMEM((256, 384), jnp.float32),
            pltpu.SemaphoreType.DMA((2 * sum(groups),)),
        ],
        compiler_params=pltpu.CompilerParams(vmem_limit_bytes=60 * 1024 * 1024),
        name="sums",
    )(panel, slab)


CHUNKS = 8


def finish_kernel(s_ref, panel, slab, l_hbm, coup_hbm, rem_hbm,
                  l_ref, coup_ref, rem, x, t, r, u, sems):
    lane = lax.broadcasted_iota(jnp.int32, (64, 128), 1)
    sub = lax.broadcasted_iota(jnp.int32, (64, 128), 0)
    low = lane < 64
    eyes = [(lane == sub).astype(jnp.float32), (lane == sub + 64).astype(jnp.float32)]
    x[0:64, 0:256] = s_ref[:, 0:256]
    x[64:128, 128:256] = s_ref[:, 256:384]
    x[64:128, 0:128] = s_ref[:, 512:640]
    x[128:192, 128:256] = s_ref[:, 384:512]
    x[192:256, 128:256] = pltpu.roll(s_ref[:, 512:640], 64, 1)
    for i in range(4):
        x[64 * i : 64 * i + 64, 256:384] = s_ref[:, 640 + 128 * i : 768 + 128 * i]
        for j in range(2):
            x[64 * i : 64 * i + 64, 384 + 128 * j : 512 + 128 * j] = eyes[i % 2] if i // 2 == j else jnp.zeros((64, 128), jnp.float32)
    r[...] = jnp.zeros_like(r)
    def keep(i, v):
        lo = 64 * i
        tile, off = lo // 128 * 128, lo % 128
        own = jnp.where((lane - off >= sub) & ((lane >= 64) == (off > 0)), v, 0.0)
        if off == 0:
            own = jnp.where(low, own, t[lo : lo + 64, tile : tile + 128])
        r[lo : lo + 64, tile : tile + 128] = own
        if tile == 0:
            r[lo : lo + 64, 128:256] = t[lo : lo + 64, 128:256]
        coup_ref[lo : lo + 64, :] = t[lo : lo + 64, 256:384]

    def solve(i, wt):
        lo, hi = 64 * i, 64 * i + 64
        start, end = hi // 128 * 128, 384 + (hi + 127) // 128 * 128
        t[lo:hi, start:end] = hdot(wt, x[lo:hi, start:end], ((1,), (0,)))

    def reduce(lo, hi, first, last, start, end):
        tile = first // 128 * 128
        down = hdot(t[lo:hi, tile : tile + 128], t[lo:hi, start:end], ((0,), (0,)))
        x[first:last, start:end] -= down[first - tile : last - tile, :]

    def backward(lo, hi):
        wide = (hi + 127) // 128 * 128
        part = hdot(t[lo:hi, 384 : 384 + wide], t[lo:hi, 256:384], ((0,), (0,)))
        if wide < 256:
            part = jnp.concatenate([part, jnp.zeros((256 - wide, 128), jnp.float32)], axis=0)
        return part

    def next_block(i, wt):
        lo, hi = 64 * i, 64 * i + 64
        tile, off = hi // 128 * 128, hi % 128
        t[lo:hi, tile : tile + 128] = hdot(wt, x[lo:hi, tile : tile + 128], ((1,), (0,)))
        ti = t[0:hi, 128:256] if i == 1 else t[lo:hi, tile : tile + 128]
        down = hdot(ti, ti, ((0,), (0,)))
        return x[hi : hi + 64, tile : tile + 128] - down[off : off + 64, :]

    d = x[0:64, 0:128]
    for i in range(4):
        m = jnp.where(low, d, eyes[1]) if i % 2 == 0 else jnp.where(low, eyes[0], d)
        eliminate(m, 64 * (i % 2), u.at[i])
        v = u[i]
        wt = v[:, 64:128] if i % 2 == 0 else v[:, 0:64]
        if i < 3:
            d = next_block(i, wt)
        solve(i, wt)
        if i == 0:
            reduce(0, 64, 64, 128, 128, 512)
        elif i == 1:
            reduce(0, 128, 128, 256, 128, 512)
            update = backward(0, 128)
        elif i == 2:
            reduce(128, 192, 192, 256, 256, 640)
            update = update + backward(128, 192)
        else:
            update = update + backward(192, 256)
        keep(i, v)
    update = update.astype(jnp.bfloat16)
    step = panel.shape[0] // CHUNKS
    share = l_ref.shape[0]
    pick = lax.broadcasted_iota(jnp.int32, (share, 256), 1) == (
        lax.broadcasted_iota(jnp.int32, (share, 256), 0) + lax.axis_index("col") * share
    )
    stores = []
    for i in range(CHUNKS):
        at = pl.ds(i * step, step)
        rem[at, :] = (
            slab[at, :].astype(jnp.float32) - jnp.dot(panel[at, :], update, preferred_element_type=jnp.float32)
        ).astype(jnp.bfloat16)
        store = pltpu.make_async_copy(rem.at[at, :], rem_hbm.at[at, :], sems.at[i])
        store.start()
        stores.append(store)
        if i == 1:
            l_ref[...] = hdot(pick.astype(jnp.float32), r[...], ((1,), (1,)))
            for n, (source, target) in enumerate(((l_ref, l_hbm), (coup_ref, coup_hbm))):
                store = pltpu.make_async_copy(source, target, sems.at[CHUNKS + n])
                store.start()
                stores.append(store)
    for store in stores:
        store.wait()


def finish(sums, panel, slab, share):
    rows = panel.shape[0]
    vmem = pl.BlockSpec(memory_space=pltpu.VMEM)
    hbm = pl.BlockSpec(memory_space=pl.ANY)
    return pl.pallas_call(
        finish_kernel,
        in_specs=[vmem, vmem, vmem],
        out_specs=(hbm, hbm, hbm),
        out_shape=(
            jax.ShapeDtypeStruct((share, 256), jnp.float32),
            jax.ShapeDtypeStruct((256, 128), jnp.float32),
            jax.ShapeDtypeStruct((rows, 128), jnp.bfloat16),
        ),
        scratch_shapes=[
            pltpu.VMEM((share, 256), jnp.float32),
            pltpu.VMEM((256, 128), jnp.float32),
            pltpu.VMEM((rows, 128), jnp.bfloat16),
            pltpu.VMEM((256, 640), jnp.float32),
            pltpu.VMEM((256, 640), jnp.float32),
            pltpu.VMEM((256, 256), jnp.float32),
            pltpu.VMEM((4, 64, 128), jnp.float32),
            pltpu.SemaphoreType.DMA((CHUNKS + 2,)),
        ],
        compiler_params=pltpu.CompilerParams(vmem_limit_bytes=24 * 1024 * 1024),
        name="finish",
    )(sums, panel, slab)


def exchange(parts):
    return lax.all_to_all(parts, "row", 0, 0, tiled=True)


def on_device(panel, slab):
    rows = lax.axis_size("row")
    parts = exchange(local_sums(panel, slab, 1.0 / (panel.shape[0] * rows)))
    mine = jnp.sum(parts, axis=0, keepdims=True)
    sums = exchange(jnp.broadcast_to(mine, parts.shape))
    share = panel.shape[1] // lax.axis_size("col")
    lower, coupling, remainder = finish(sums.reshape(rows, -1), panel, slab, share)
    return (lower.T, coupling, remainder)


def solution(mesh):
    return jax.shard_map(
        on_device,
        mesh=mesh,
        in_specs=(P("row", None), P("row", "col")),
        out_specs=(P(None, "col"), P(None, "col"), P("row", "col")),
        check_vma=False,
    )
```
